256 devices in a mesh: blk: 4 (over y_lo, core), grp: 64 (over y_hi, z, x).
Axes of the slice: x: 4, y: 4 (y_hi: 2, y_lo: 2; y = y_hi * 2 + y_lo), z: 8, core: 2. Of those that a mesh axis runs over, the one named last changes fastest.
Arguments:
- images: bfloat16 [12288, 1152], P('grp'), may hold values from -6 to 6
- texts: bfloat16 [12288, 1152], P(('blk', 'grp')), may hold values from -6 to 6
- log_temp: float32 [1], replicated, may hold values from -4 to -3
- bias: float32 [1], replicated, may hold values from -2 to 0
Outputs:
- loss: float32 [1], replicated
- grad_images: float32 [12288, 1152], P('grp')
- grad_texts: float32 [12288, 1152], P(('blk', 'grp'))
- grad_log_temp: float32 [1], replicated
- grad_bias: float32 [1], replicated
The draws below stay inside these ranges and needn't reach their ends.
All inputs are finite; a program needn't handle non-finite values.
Results may differ from the reference program's by a relative error of at most 0.001.
The reference program's roundings to bfloat16 on the way (of `coef`) count: a program that leaves them out, or rounds other values in their place, can miss the bound.
Values may be sent and summed in bfloat16 or wider, within the bound.
A program may use at most 64 MiB of HBM per device.

```python
import jax
import jax.numpy as jnp
from jax import lax

D = 1152
BATCH = 12288


def levels(own_key, extent, pieces, smallest, top_value):
    def one(dim, shards_of):
        steps = jax.random.uniform(jax.random.fold_in(jax.random.fold_in(own_key, 6), dim), (shards_of,), jnp.float32, smallest / len(pieces), top_value / len(pieces))
        return jnp.repeat(jnp.exp(steps), extent[dim] // shards_of).reshape((-1,) + (1,) * (len(extent) - dim - 1))

    gain = one(*pieces[0])
    for cut in pieces[1:]:
        gain = gain * one(*cut)
    return gain


def gaussian(rng, dims, scale, bound, pieces=(), kind=jnp.bfloat16):
    array = scale * jax.random.normal(rng, dims, jnp.float32)
    if pieces:
        array = array * levels(rng, dims, pieces, -0.22, 0.18)
    return jnp.clip(array, -bound, bound).astype(kind)


def setup_inputs(seed: int = 0) -> dict:
    arg_keys = jax.random.split(jax.random.key(seed), 5)
    images = gaussian(arg_keys[0], (BATCH, D), 1.0, 6.0, ((0, 64),))
    texts = gaussian(arg_keys[1], (BATCH, D), 1.0, 6.0, ((0, 256),))
    log_temp = jnp.clip(jax.random.uniform(arg_keys[2], (1,), jnp.float32, -4.0, -3.0), -4.0, -3.0)
    bias = jnp.clip(jax.random.uniform(arg_keys[3], (1,), jnp.float32, -2.0, 0.0), -2.0, 0.0)
    return dict(images=images, texts=texts, log_temp=log_temp, bias=bias)


def reference(images, texts, log_temp, bias):
    scale = jnp.exp(log_temp[0])
    shift_b = bias[0]
    total = images.shape[0]
    rows_blk = min(512, total)
    nblocks = total // rows_blk
    columns = jnp.arange(total, dtype=jnp.int32)

    def step(carry, index):
        grad_txt, loss_sum, temp_sum, bias_sum = carry
        start = (index * rows_blk).astype(jnp.int32)
        part = lax.dynamic_slice_in_dim(images, start, rows_blk, 0)
        logits = scale * jnp.dot(part, texts.T, preferred_element_type=jnp.float32) + shift_b
        row_ids = start + jnp.arange(rows_blk, dtype=jnp.int32)
        sign = jnp.where(row_ids[:, None] == columns[None, :], 1.0, -1.0).astype(jnp.float32)
        term = jax.nn.log_sigmoid(sign * logits)
        dlogit = -sign * jax.nn.sigmoid(-sign * logits)
        coef = (scale * dlogit).astype(jnp.bfloat16)
        grad_img = jnp.dot(coef, texts, preferred_element_type=jnp.float32)
        grad_txt = grad_txt + jnp.dot(coef.T, part, preferred_element_type=jnp.float32)
        carry = (grad_txt, loss_sum - jnp.sum(term), temp_sum + jnp.sum(dlogit * (logits - shift_b)), bias_sum + jnp.sum(dlogit))
        return carry, grad_img

    start_carry = (jnp.zeros(texts.shape, jnp.float32), jnp.float32(0.0), jnp.float32(0.0), jnp.float32(0.0))
    final, grad_blocks = lax.scan(step, start_carry, jnp.arange(nblocks, dtype=jnp.int32))
    grad_txt, loss_sum, temp_sum, bias_sum = final
    grad_img = grad_blocks.reshape(total, images.shape[1])
    count = jnp.float32(total) * jnp.float32(total)
    return (jnp.reshape(loss_sum / count, (1,)), grad_img, grad_txt,
            jnp.reshape(temp_sum / count, (1,)), jnp.reshape(bias_sum / count, (1,)))
```

```python
import functools

import jax
import jax.numpy as jnp
from jax import lax
from jax.experimental import pallas as pl
from jax.experimental.pallas import tpu as pltpu
from jax.sharding import PartitionSpec as P

MESH = pl.DeviceIdType.MESH
F32 = jnp.float32
BF16 = jnp.bfloat16

ROWS = 48
D = 1152
NX, NY, NZ = 4, 4, 8
SIDE = 16 * ROWS
SUB = 16

GROUPS = ((4, 3, 5), (2, 6), (1, 7, 0))
LOW, HIGH = 2.0**-6, 2.0**6 - 2.0**-6


def text_row(rel, other):
    base = 0
    for group in GROUPS:
        if rel in group:
            return base + (other * len(group) + group.index(rel)) * ROWS
        base += 2 * len(group) * ROWS
    raise ValueError(rel)


def encode(value):
    rows = value.shape[0]
    magnitude = jnp.abs(value)
    tall = jnp.max(magnitude.reshape(rows // 8, 8, D), axis=0)
    top = tall[:, :128]
    for i in range(1, D // 128):
        top = jnp.maximum(top, tall[:, 128 * i : 128 * i + 128])
    top = jnp.maximum(top, 1e-30)
    gain = jnp.concatenate([HIGH / top] * (D // 128), axis=1)
    t = magnitude.reshape(rows // 8, 8, D) * gain[None] + LOW
    for _ in range(4):
        t = t * t
    t = t.reshape(rows, D)
    return jnp.where(value < 0, -t, t).astype(BF16), top


def decode(code, top):
    rows = code.shape[0]
    v = code.astype(F32)
    gain = jnp.concatenate([top * (1.0 / HIGH)] * (D // 128), axis=1)
    t = jnp.exp2(jnp.log2(jnp.abs(v)) * 0.0625) - LOW
    t = (t.reshape(rows // 8, 8, D) * gain[None]).reshape(rows, D)
    return jnp.where(v < 0, -t, t)


def kernel(img, txt, lt, bs, loss_o, gimg_o, gtxt_o, temp_o, bias_o,
           I, T, PM, L, GI, GT, RT, rid, cid,
           ac_s, am_s, ac_r, am_r, zc_s, zm_s, zc_r, zm_r,
           sc_s, sc_x, sc_y, sc_z, sc_c, acc, ss, rs, ls):
    blk, grp = lax.axis_index("blk"), lax.axis_index("grp")
    lo, c = lax.div(blk, 2), lax.rem(blk, 2)
    h, z, x = lax.div(grp, 32), lax.rem(lax.div(grp, 4), 8), lax.rem(grp, 4)
    y = 2 * h + lo
    s = 1 - 2 * c

    def dev(x, y, z, c):
        return (lax.rem(y, 2) * 2 + c, lax.div(y, 2) * 32 + z * 4 + x)

    def at_x(d):
        return dev(lax.rem(x + d, 4), y, z, c)

    def at_y(d):
        return dev(x, lax.rem(y + d, 4), z, c)

    def at_z(d):
        return dev(x, y, lax.rem(z + s * d + 8, 8), c)

    def at_a(d):
        return dev(lax.rem(x + d * (1 - c), 4), lax.rem(y + d * c, 4), z, c)

    def at_b(d):
        return dev(lax.rem(x + d * c, 4), lax.rem(y + d * (1 - c), 4), z, c)

    at_core = dev(x, y, z, 1 - c)
    dyt, dyf = 1 + 2 * lo, 3 - 2 * lo

    barrier = pltpu.get_barrier_semaphore()
    peers = [at_x(1), at_x(2), at_x(3), at_y(1), at_y(2), at_y(3)] + [at_z(d) for d in range(1, 8)] + [at_core]
    for peer in peers:
        pl.semaphore_signal(barrier, inc=1, device_id=peer, device_id_type=MESH)

    def slot(dx, dy):
        return (dx * (1 + 3 * c) + dy * (4 - 3 * c)) * ROWS

    def rows_at(start, n, unit=ROWS):
        return pl.ds(pl.multiple_of(start, unit), n)

    mine = []
    for k, (dy, q) in enumerate(((0, lo), (dyt, 1 - lo))):
        mine.append(pltpu.make_async_copy(
            img.at[rows_at((q * 2 + c) * ROWS, ROWS)], I.at[rows_at(slot(0, dy), ROWS)], ls.at[k]))
    mine.append(pltpu.make_async_copy(txt, T.at[pl.ds(text_row(0, 0), ROWS)], ls.at[2]))
    for copy in mine:
        copy.start()

    for dy in range(4):
        for dx in range(4):
            x2, y2 = lax.rem(x + dx, 4), lax.rem(y + dy, 4)
            first = (lax.div(y2, 2) * 32 + z * 4 + x2) * 192 + (lax.rem(y2, 2) * 2 + c) * ROWS
            rid[rows_at(slot(dx, dy), ROWS), :] = first + lax.broadcasted_iota(jnp.int32, (ROWS, 128), 0)
    lane = lax.broadcasted_iota(jnp.int32, (8, SIDE), 1)
    ids = jnp.zeros((8, SIDE), jnp.int32)
    for rel in range(8):
        for other in range(2):
            z2 = lax.rem(z + (s if other == 0 else -s) * rel + 8, 8)
            c2 = c if other == 0 else 1 - c
            row = text_row(rel, other)
            first = (lo * 2 + c2) * 3072 + (h * 32 + z2 * 4 + x) * ROWS - row
            ids = jnp.where((lane >= row) & (lane < row + ROWS), lane + first, ids)
    cid[...] = ids
    acc[...] = jnp.zeros_like(acc)
    scale = jnp.exp(jnp.full((1, 128), lt[0], F32))
    shift = bs[0]

    pl.semaphore_wait(barrier, len(peers))

    sent = []
    count = [0]

    def send(src, dst, device):
        k = count[0]
        count[0] += 1
        copy = pltpu.make_async_remote_copy(
            src_ref=src, dst_ref=dst, send_sem=ss.at[k], recv_sem=rs.at[k], device_id=device, device_id_type=MESH)
        copy.start()
        sent.append(copy)
        return copy

    def send_piece(src, src_row, dst, dst_row, device, subs=3):
        n = ROWS // subs
        return [send(src.at[rows_at(src_row + i * n, n, n)], dst.at[rows_at(dst_row + i * n, n, n)], device)
                for i in range(subs)]

    def wait(copies):
        for copy in copies:
            copy.wait_recv()

    own_row, twin_row = (lo * 2 + c) * ROWS, ((1 - lo) * 2 + c) * ROWS
    t_p = {0: send_piece(txt, 0, T, text_row(7, 0), at_z(1))}
    t_m = {0: send_piece(txt, 0, T, text_row(1, 0), at_z(7))}
    xp0 = send_piece(img, own_row, I, slot(3, 0), at_x(1))
    xm1 = send_piece(img, twin_row, I, slot(1, dyt), at_x(3))
    yf0 = send_piece(img, own_row, I, slot(0, dyt), at_y(dyf))
    xp1 = send_piece(img, twin_row, I, slot(3, dyt), at_x(1))
    xm0 = send_piece(img, own_row, I, slot(1, 0), at_x(3))
    t_c = {0: send_piece(txt, 0, T, text_row(0, 1), at_core, 1)}

    xpf, xmf, y1, y2, y3, w0, w1, w2, w3 = [], [], [], [], [], [], [], [], []
    dxs, dxi = 1 + 2 * lo, 3 - 2 * lo

    def forward(copies, i, src, src_row, dst, dst_row, device, out):
        copies[i].wait_recv()
        out.append(send(src.at[rows_at(src_row + i * SUB, SUB, SUB)], dst.at[rows_at(dst_row + i * SUB, SUB, SUB)], device))

    def text_step(k):
        t_p[k], t_m[k] = [], []
        for i in range(3):
            forward(t_p[k - 1], i, T, text_row(8 - k, 0), T, text_row(7 - k, 0), at_z(1), t_p[k])
            if k < 3:
                forward(t_m[k - 1], i, T, text_row(k, 0), T, text_row(k + 1, 0), at_z(7), t_m[k])
        if k == 3:
            wait(t_m[2])
        t_c[8 - k] = send_piece(T, text_row(8 - k, 0), T, text_row(8 - k, 1), at_core, 1)
        t_c[k] = send_piece(T, text_row(k, 0), T, text_row(k, 1), at_core, 1)

    for i in range(3):
        forward(xp0, i, I, slot(3, 0), I, slot(2, 0), at_x(1), xpf)
        forward(xm1, i, I, slot(1, dyt), I, slot(2, dyt), at_x(3), xmf)
        forward(yf0, i, I, slot(0, dyf), I, slot(0, 2), at_y(dyt), w0)
    text_step(1)
    wait(xm0)
    for i in range(3):
        y1.append(send(I.at[rows_at(slot(dxs, 0) + i * SUB, SUB, SUB)],
                       I.at[rows_at(slot(dxs, dyt) + i * SUB, SUB, SUB)], at_y(dyf)))
    wait(xp1)
    for i in range(3):
        y2.append(send(I.at[rows_at(slot(dxs, dyt) + i * SUB, SUB, SUB)],
                       I.at[rows_at(slot(dxs, 2) + i * SUB, SUB, SUB)], at_y(dyf)))
    text_step(2)
    for i in range(3):
        forward(y1, i, I, slot(dxi, dyf), I, slot(dxi, 2), at_y(dyt), w1)
    for i in range(3):
        forward(xpf, i, I, slot(2, 0), I, slot(2, dyt), at_y(dyf), y3)
    text_step(3)
    for i in range(3):
        forward(y2, i, I, slot(dxi, 2), I, slot(dxi, dyt), at_y(dyt), w2)
    for i in range(3):
        forward(y3, i, I, slot(2, dyf), I, slot(2, 2), at_y(dyt), w3)
    wait(t_p[3])
    t_c[4] = send_piece(T, text_row(4, 0), T, text_row(4, 1), at_core, 1)
    for rel in range(8):
        wait(t_c[rel])
    for copy in mine:
        copy.wait()
    wait(xmf)
    for copies in (w0, w1, w2, w3):
        wait(copies)

    def pair(g):
        base = g * (4 * ROWS)
        L[...] = lax.dot_general(I[rows_at(base, 4 * ROWS), :], T[...], (((1,), (1,)), ((), ())),
                                 preferred_element_type=F32)

        def chunk(i, carry):
            r = pl.multiple_of(i * 16, 16)
            rg = pl.multiple_of(base + i * 16, 16)
            rows = rid[pl.ds(rg, 16), :]
            sums = list(carry)
            for j in range(0, SIDE, 384):
                dot = L[pl.ds(r, 16), j : j + 384] * jnp.concatenate([scale] * 3, axis=1)
                same = jnp.concatenate([rows] * 3, axis=1) == jnp.concatenate([cid[:, j : j + 384]] * 2, axis=0)
                logit = dot + shift
                signed = jnp.where(same, logit, -logit)
                e = jnp.exp(-jnp.abs(signed))
                inv = 1.0 / (1.0 + e)
                term = jnp.minimum(signed, 0.0) - jnp.log1p(e)
                d = jnp.where(signed >= 0, e, 1.0) * inv
                d = jnp.where(same, -d, d)
                PM[pl.ds(rg, 16), j : j + 384] = (d * jnp.concatenate([scale] * 3, axis=1)).astype(BF16)
                for n, v in enumerate((term, d * dot, d)):
                    for q in range(3):
                        w = v[:, 128 * q : 128 * q + 128]
                        sums[n] = sums[n] + (w[:8] + w[8:])
            return tuple(sums)

        zero = jnp.zeros((8, 128), F32)
        sums = lax.fori_loop(0, 12, chunk, (zero, zero, zero))
        for n in range(3):
            acc[8 * n : 8 * n + 8, :] += sums[n]
        GI[rows_at(base, 4 * ROWS), :] = jnp.dot(PM[rows_at(base, 4 * ROWS), :], T[...], preferred_element_type=F32)

    def send_code(k, row, device, dst=None):
        code, top = encode(GI[rows_at(row, ROWS), :])
        ac_s[k] = code
        am_s[k] = top
        dst = k if dst is None else dst
        return [send(ac_s.at[k], ac_r.at[dst], device), send(am_s.at[k], am_r.at[dst], device)]

    def got(k):
        return decode(ac_r[k], am_r[k])

    g1 = (1 + 2 * lo) * (1 - c) + c
    order = (0, g1, 4 - g1, 2)
    a2, am, ap, bb = {}, {}, {}, {}

    def first_sends(i):
        base = order[i] * (4 * ROWS)
        d = 1 if i % 2 == 0 else 3
        a2[i] = send_code(3 * i, base + 2 * ROWS, at_a(d))
        am[i] = send_code(3 * i + 1, base + (4 - d) * ROWS, at_a(4 - d))

    def add_on(i):
        base = order[i] * (4 * ROWS)
        d = 1 if i % 2 == 0 else 3
        wait(a2[i])
        GI[rows_at(base + d * ROWS, ROWS), :] += got(3 * i)
        ap[i] = send_code(3 * i + 2, base + d * ROWS, at_a(d))

    def close(i):
        base = order[i] * (4 * ROWS)
        wait(am[i])
        wait(ap[i])
        GI[rows_at(base, ROWS), :] += got(3 * i + 1) + got(3 * i + 2)
        if i == 0:
            return
        code, top = encode(GI[rows_at(base, ROWS), :])
        ac_s[11 + i] = code
        am_s[11 + i] = top
        g = order[i]
        if i == 3:
            bb[3] = [send(ac_s.at[14], ac_r.at[14], at_b(2)), send(am_s.at[14], am_r.at[14], at_b(2))]
        else:
            k = 12 + lax.div(g, 2)
            base_k = count[0] if i == 1 else bb["k"]
            if i == 1:
                bb["k"] = base_k
                count[0] += 4
            copies = []
            for n, (src, dst) in enumerate(((ac_s, ac_r), (am_s, am_r))):
                sem = base_k + 2 * n + lax.div(g, 2)
                copy = pltpu.make_async_remote_copy(
                    src_ref=src.at[11 + i], dst_ref=dst.at[k], send_sem=ss.at[sem], recv_sem=rs.at[sem],
                    device_id=at_b(g), device_id_type=MESH)
                copy.start()
                sent.append(copy)
                copies.append(copy)
            bb[i] = copies

    cores = {}

    def text_grads(g):
        n = len(GROUPS[g]) * ROWS
        base = text_row(GROUPS[g][0], 0)
        GT[pl.ds(base, 2 * n), :] = lax.dot_general(PM[:, base : base + 2 * n], I[...], (((0,), (0,)), ((), ())),
                                                    preferred_element_type=F32)
        half = text_half(g)
        cores[g] = send(GT.at[pl.ds(base + n, n)], RT.at[pl.ds(half, n)], at_core)

    def text_half(g):
        return sum(len(GROUPS[i]) for i in range(g)) * ROWS

    def text_join(g):
        n = len(GROUPS[g]) * ROWS
        base = text_row(GROUPS[g][0], 0)
        cores[g].wait_recv()
        GT[pl.ds(base, n), :] += RT[pl.ds(text_half(g), n), :]

    zs = {}

    def z_send(chain, step, i, rel, incoming):
        row = text_row(rel, 0) + i * SUB
        value = GT[row : row + SUB, :]
        k = ((0 if chain == "p" else 4) + step) * 3 + i
        if incoming:
            wait(zs[chain, step - 1, i])
            value = value + decode(zc_r[k - 3], zm_r[k - 3])
        code, top = encode(value)
        zc_s[k] = code
        zm_s[k] = top
        device = at_z(1) if chain == "p" else at_z(7)
        zs[chain, step, i] = [send(zc_s.at[k], zc_r.at[k], device), send(zm_s.at[k], zm_r.at[k], device)]

    for i in range(4):
        pair(order[i])
        first_sends(i)
        if i:
            add_on(i - 1)
    sc_s[0] = acc[...]
    sc = {"c": send(sc_s.at[0], sc_c, at_core)}
    text_grads(0)
    add_on(3)
    text_join(0)
    for i in range(3):
        z_send("p", 0, i, 4, False)
        z_send("m", 0, i, 5, False)
    text_grads(1)
    close(0)
    close(1)
    sc["c"].wait_recv()
    sc_s[1] = sc_s[0] + sc_c[...]
    sc_x[x] = sc_s[1]
    sc["x"] = [send(sc_s.at[1], sc_x.at[x], at_x(d)) for d in (1, 2, 3)]
    for i in range(3):
        z_send("p", 1, i, 3, True)
    text_join(1)
    for i in range(3):
        z_send("m", 1, i, 6, True)
    text_grads(2)
    close(2)
    wait(sc["x"])
    sc_s[2] = (sc_x[0] + sc_x[1]) + (sc_x[2] + sc_x[3])
    sc_y[y] = sc_s[2]
    sc["y"] = [send(sc_s.at[2], sc_y.at[y], at_y(d)) for d in (1, 2, 3)]
    for i in range(3):
        z_send("p", 2, i, 2, True)
    text_join(2)
    for i in range(3):
        z_send("m", 2, i, 7, True)
    close(3)
    wait(sc["y"])
    sc_s[3] = (sc_y[0] + sc_y[1]) + (sc_y[2] + sc_y[3])
    sc_z[z] = sc_s[3]
    sc["z"] = [send(sc_s.at[3], sc_z.at[z], at_z(d)) for d in range(1, 8)]
    for i in range(3):
        z_send("p", 3, i, 1, True)
    for i in (1, 2, 3):
        wait(bb[i])
    GI[0:ROWS, :] += got(12) + got(13) + got(14)
    code, top = encode(GI[0:ROWS, :])
    ac_s[15] = code
    am_s[15] = top
    twin = [send(ac_s.at[15], ac_r.at[15], at_y(dyt)), send(am_s.at[15], am_r.at[15], at_y(dyt))]
    side = [send(ac_s.at[15], ac_r.at[16], at_core), send(am_s.at[15], am_r.at[16], at_core)]
    gimg_o[rows_at(own_row, ROWS), :] = decode(code, top)
    for i in range(3):
        row = text_row(0, 0) + i * SUB
        wait(zs["p", 3, i])
        wait(zs["m", 2, i])
        kp, km = 3 * 3 + i, 6 * 3 + i
        gtxt_o[i * SUB : i * SUB + SUB, :] = (GT[row : row + SUB, :] + decode(zc_r[kp], zm_r[kp])
                                              + decode(zc_r[km], zm_r[km]))
    wait(sc["z"])
    total = sc_z[0]
    for i in range(1, 8):
        total = total + sc_z[i]
    pairs = 1.0 / (256.0 * ROWS * 256.0 * ROWS)
    loss_o[0] = -jnp.sum(total[0:8]) * pairs
    temp_o[0] = jnp.sum(total[8:16]) * pairs
    bias_o[0] = jnp.sum(total[16:24]) * pairs
    wait(twin)
    pair_side = [send(ac_r.at[15], ac_r.at[17], at_core), send(am_r.at[15], am_r.at[17], at_core)]
    gimg_o[rows_at(twin_row, ROWS), :] = got(15)
    wait(side)
    gimg_o[rows_at((lo * 2 + 1 - c) * ROWS, ROWS), :] = got(16)
    wait(pair_side)
    gimg_o[rows_at(((1 - lo) * 2 + 1 - c) * ROWS, ROWS), :] = got(17)
    for copy in sent:
        copy.wait_send()


def local(images, texts, log_temp, bias):
    sems = 220
    vmem = pl.BlockSpec(memory_space=pltpu.VMEM)
    smem = pl.BlockSpec(memory_space=pltpu.SMEM)
    hbm = pl.BlockSpec(memory_space=pl.ANY)
    scalar = jax.ShapeDtypeStruct((1,), F32)
    V = pltpu.VMEM
    return pl.pallas_call(
        kernel,
        out_shape=(scalar, jax.ShapeDtypeStruct((4 * ROWS, D), F32), jax.ShapeDtypeStruct((ROWS, D), F32), scalar, scalar),
        in_specs=[hbm, hbm, smem, smem],
        out_specs=(smem, vmem, vmem, smem, smem),
        scratch_shapes=[
            V((SIDE, D), BF16), V((SIDE, D), BF16), V((SIDE, SIDE), BF16), V((4 * ROWS, SIDE), F32),
            V((SIDE, D), F32), V((SIDE, D), F32), V((SIDE // 2, D), F32),
            V((SIDE, 128), jnp.int32), V((8, SIDE), jnp.int32),
            V((16, ROWS, D), BF16), V((16, 8, 128), F32), V((18, ROWS, D), BF16), V((18, 8, 128), F32),
            V((21, SUB, D), BF16), V((21, 8, 128), F32), V((21, SUB, D), BF16), V((21, 8, 128), F32),
            V((4, 24, 128), F32), V((4, 24, 128), F32), V((4, 24, 128), F32), V((8, 24, 128), F32),
            V((24, 128), F32), V((24, 128), F32),
            pltpu.SemaphoreType.DMA((sems,)), pltpu.SemaphoreType.DMA((sems,)), pltpu.SemaphoreType.DMA((3,)),
        ],
        compiler_params=pltpu.CompilerParams(collective_id=0, has_side_effects=True, vmem_limit_bytes=48 << 20),
        name="pairs",
    )(images, texts, log_temp, bias)


def solution(mesh):
    return jax.shard_map(
        local,
        mesh=mesh,
        in_specs=(P("grp", None), P(("blk", "grp"), None), P(), P()),
        out_specs=(P(), P("grp", None), P(("blk", "grp"), None), P(), P()),
        check_vma=False,
    )
```

```python
import functools

import jax
import jax.numpy as jnp
from jax import lax
from jax.experimental import pallas as pl
from jax.experimental.pallas import tpu as pltpu
from jax.sharding import PartitionSpec as P

MESH = pl.DeviceIdType.MESH
F32 = jnp.float32
BF16 = jnp.bfloat16

ROWS = 48
D = 1152
NX, NY, NZ = 4, 4, 8
SIDE = 16 * ROWS
SUB = 16
HALF = SIDE // 2

GROUPS = ((4, 3, 5), (2, 6), (1, 7, 0))
LOW, HIGH = 2.0**-6, 2.0**6 - 2.0**-6


def text_row(rel, other):
    base = 0
    for group in GROUPS:
        if rel in group:
            return base + (other * len(group) + group.index(rel)) * ROWS
        base += 2 * len(group) * ROWS
    raise ValueError(rel)


def encode(value, message):
    tiles = [(r, j) for r in range(0, value.shape[0], 16) for j in range(0, D, 128)]
    top = jnp.full((16, 128), 1e-30, F32)
    for r, j in tiles:
        top = jnp.maximum(top, jnp.abs(value[r : r + 16, j : j + 128]))
    top = (top * 1.004).astype(BF16)
    gain = HIGH / top.astype(F32)
    for n, (r, j) in enumerate(tiles):
        v = value[r : r + 16, j : j + 128]
        t = jnp.abs(v) * gain + LOW
        for _ in range(4):
            t = t * t
        message[n] = jnp.where(v < 0, -t, t).astype(BF16)
    message[len(tiles)] = top


def decode(message, rows):
    count = rows // 16 * (D // 128)
    gain = message[count].astype(F32) * (1.0 / HIGH)
    out = []
    for n in range(count):
        v = message[n].astype(F32)
        t = (jnp.exp2(jnp.log2(jnp.abs(v)) * 0.0625) - LOW) * gain
        out.append(jnp.where(v < 0, -t, t))
    width = D // 128
    return jnp.concatenate(
        [jnp.concatenate(out[i : i + width], axis=1) for i in range(0, count, width)], axis=0)


def kernel(img, txt, lt, bs, loss_o, gimg_o, gtxt_o, temp_o, bias_o,
           I, T, PM, L, GI, GT, RT, rid, cid,
           img_s, img_r, txt_s, txt_r,
           sc_s, sc_x, sc_y, sc_z, sc_c, acc, ss, rs, ls):
    blk, grp = lax.axis_index("blk"), lax.axis_index("grp")
    lo, c = lax.div(blk, 2), lax.rem(blk, 2)
    h, z, x = lax.div(grp, 32), lax.rem(lax.div(grp, 4), 8), lax.rem(grp, 4)
    y = 2 * h + lo
    s = 1 - 2 * c

    def dev(x, y, z, c):
        return (lax.rem(y, 2) * 2 + c, lax.div(y, 2) * 32 + z * 4 + x)

    def at_x(d):
        return dev(lax.rem(x + d, 4), y, z, c)

    def at_y(d):
        return dev(x, lax.rem(y + d, 4), z, c)

    def at_z(d):
        return dev(x, y, lax.rem(z + s * d + 8, 8), c)

    def at_a(d):
        return dev(lax.rem(x + d * (1 - c), 4), lax.rem(y + d * c, 4), z, c)

    def at_b(d):
        return dev(lax.rem(x + d * c, 4), lax.rem(y + d * (1 - c), 4), z, c)

    at_core = dev(x, y, z, 1 - c)
    dyt, dyf = 1 + 2 * lo, 3 - 2 * lo

    barrier = pltpu.get_barrier_semaphore()
    peers = [at_x(1), at_x(2), at_x(3), at_y(1), at_y(2), at_y(3)] + [at_z(d) for d in range(1, 8)]
    peers += [at_core]
    for peer in peers:
        pl.semaphore_signal(barrier, inc=1, device_id=peer, device_id_type=MESH)

    def slot(dx, dy):
        return (dx * (1 + 3 * c) + dy * (4 - 3 * c)) * ROWS

    def rows_at(start, n, unit=ROWS):
        return pl.ds(pl.multiple_of(start, unit), n)

    mine = []
    for k, (dy, q) in enumerate(((0, lo), (dyt, 1 - lo))):
        mine.append(pltpu.make_async_copy(
            img.at[rows_at((q * 2 + c) * ROWS, ROWS)], I.at[rows_at(slot(0, dy), ROWS)], ls.at[k]))
    mine.append(pltpu.make_async_copy(txt, T.at[pl.ds(text_row(0, 0), ROWS)], ls.at[2]))
    for copy in mine:
        copy.start()

    for dy in range(4):
        for dx in range(4):
            x2, y2 = lax.rem(x + dx, 4), lax.rem(y + dy, 4)
            first = (lax.div(y2, 2) * 32 + z * 4 + x2) * 192 + (lax.rem(y2, 2) * 2 + c) * ROWS
            rid[rows_at(slot(dx, dy), ROWS), :] = first + lax.broadcasted_iota(jnp.int32, (ROWS, 128), 0)
    lane = lax.broadcasted_iota(jnp.int32, (8, SIDE), 1)
    ids = jnp.zeros((8, SIDE), jnp.int32)
    for rel in range(8):
        for other in range(2):
            z2 = lax.rem(z + (s if other == 0 else -s) * rel + 8, 8)
            c2 = c if other == 0 else 1 - c
            row = text_row(rel, other)
            first = (lo * 2 + c2) * 3072 + (h * 32 + z2 * 4 + x) * ROWS - row
            ids = jnp.where((lane >= row) & (lane < row + ROWS), lane + first, ids)
    cid[...] = ids
    acc[...] = jnp.zeros_like(acc)
    scale = jnp.exp(jnp.full((1, 128), lt[0], F32))
    shift = bs[0]

    pl.semaphore_wait(barrier, len(peers))

    sent = []
    count = [0]

    def send(src, dst, device, sem=None):
        k = count[0] if sem is None else sem
        if sem is None:
            count[0] += 1
        copy = pltpu.make_async_remote_copy(
            src_ref=src, dst_ref=dst, send_sem=ss.at[k], recv_sem=rs.at[k], device_id=device, device_id_type=MESH)
        copy.start()
        sent.append(copy)
        return copy

    def send_piece(src, src_row, dst, dst_row, device, subs=3):
        n = ROWS // subs
        return [send(src.at[rows_at(src_row + i * n, n, n)], dst.at[rows_at(dst_row + i * n, n, n)], device)
                for i in range(subs)]

    def wait(copies):
        for copy in copies:
            copy.wait_recv()

    own_row, twin_row = (lo * 2 + c) * ROWS, ((1 - lo) * 2 + c) * ROWS
    dxs, dxi = 1 + 2 * lo, 3 - 2 * lo

    def hop(src, src_row, dst, dst_row, i, device):
        return send(src.at[rows_at(src_row + i * SUB, SUB, SUB)], dst.at[rows_at(dst_row + i * SUB, SUB, SUB)], device)

    def text_hop(rel, into, i, distance):
        return hop(T, text_row(rel, 0), T, text_row(into, 0), i, at_z(distance))

    t7, t1, t6, t2, t5, t4, t3 = [], [], [], [], [], [], []
    xp0, xm1, xp1, xm0, yf0 = [], [], [], [], []
    for i in range(3):
        t7.append(hop(txt, 0, T, text_row(7, 0), i, at_z(1)))
        t1.append(hop(txt, 0, T, text_row(1, 0), i, at_z(7)))
        xp0.append(hop(img, own_row, I, slot(3, 0), i, at_x(1)))
        xm1.append(hop(img, twin_row, I, slot(1, dyt), i, at_x(3)))
        yf0.append(hop(img, own_row, I, slot(0, dyt), i, at_y(dyf)))
    for i in range(3):
        xp1.append(hop(img, twin_row, I, slot(3, dyt), i, at_x(1)))
        xm0.append(hop(img, own_row, I, slot(1, 0), i, at_x(3)))
    t_c = [send_piece(txt, 0, T, text_row(0, 1), at_core, 1)]

    xpf, xmf, y1, y2, w0, w1, w2, v1, v2 = [], [], [], [], [], [], [], [], []
    for i in range(3):
        t7[i].wait_recv()
        t6.append(text_hop(7, 6, i, 1))
        t1[i].wait_recv()
        t2.append(text_hop(1, 2, i, 7))
        xp0[i].wait_recv()
        xm1[i].wait_recv()
        y1.append(hop(I, slot(dxs, 1 - lo), I, slot(dxs, 2 + lo), i, at_y(dyf)))
        xpf.append(hop(I, slot(3, 0), I, slot(2, 0), i, at_x(1)))
        xmf.append(hop(I, slot(1, dyt), I, slot(2, dyt), i, at_x(3)))
        yf0[i].wait_recv()
        w0.append(hop(I, slot(0, dyf), I, slot(0, 2), i, at_y(dyt)))
    t_c.append(send_piece(T, text_row(7, 0), T, text_row(7, 1), at_core, 1))
    t_c.append(send_piece(T, text_row(1, 0), T, text_row(1, 1), at_core, 1))
    for i in range(3):
        xp1[i].wait_recv()
        xm0[i].wait_recv()
        y2.append(hop(I, slot(dxs, 3 * lo), I, slot(dxs, 1 + lo), i, at_y(dyf)))
    for i in range(3):
        y1[i].wait_recv()
        w1.append(hop(I, slot(dxi, 3 - lo), I, slot(dxi, 2 + lo), i, at_y(dyt)))
        v1.append(hop(I, slot(dxi, 3 - lo), I, slot(2, 3 - lo), i, at_x(dxs)))
        t6[i].wait_recv()
        t5.append(text_hop(6, 5, i, 1))
        t4.append(text_hop(6, 4, i, 2))
        t2[i].wait_recv()
        t3.append(text_hop(2, 3, i, 7))
    t_c.append(send_piece(T, text_row(6, 0), T, text_row(6, 1), at_core, 1))
    t_c.append(send_piece(T, text_row(2, 0), T, text_row(2, 1), at_core, 1))
    for i in range(3):
        y2[i].wait_recv()
        w2.append(hop(I, slot(dxi, 2 - lo), I, slot(dxi, 1 + lo), i, at_y(dyt)))
        v2.append(hop(I, slot(dxi, 2 - lo), I, slot(2, 2 - lo), i, at_x(dxs)))
    for i in range(3):
        for rel, copies in ((3, t3), (5, t5)):
            copies[i].wait_recv()
            t_c.append([hop(T, text_row(rel, 0), T, text_row(rel, 1), i, at_core)])
    for i in range(3):
        t4[i].wait_recv()
        t_c.append([hop(T, text_row(4, 0), T, text_row(4, 1), i, at_core)])
    for copies in t_c:
        wait(copies)
    for copy in mine:
        copy.wait()
    for copies in (xpf, xmf, w0, w1, w2, v1, v2):
        wait(copies)

    g1 = (1 + 2 * lo) * (1 - c) + c
    order = (2, g1, 4 - g1, 0)

    def pair(g, j):
        base = order[g] * (4 * ROWS)
        L[...] = lax.dot_general(I[rows_at(base, 4 * ROWS), :], T[j : j + HALF, :], (((1,), (1,)), ((), ())),
                                 preferred_element_type=F32)

        def chunk(i, carry):
            r = pl.multiple_of(i * 16, 16)
            rg = pl.multiple_of(base + i * 16, 16)
            rows = rid[pl.ds(rg, 16), :]
            sums = list(carry)
            dot = L[pl.ds(r, 16), :] * jnp.concatenate([scale] * 3, axis=1)
            same = jnp.concatenate([rows] * 3, axis=1) == jnp.concatenate([cid[:, j : j + HALF]] * 2, axis=0)
            logit = dot + shift
            signed = jnp.where(same, logit, -logit)
            e = jnp.exp(-jnp.abs(signed))
            inv = 1.0 / (1.0 + e)
            term = jnp.minimum(signed, 0.0) - jnp.log1p(e)
            d = jnp.where(signed >= 0, e, 1.0) * inv
            d = jnp.where(same, -d, d)
            PM[pl.ds(rg, 16), j : j + HALF] = (d * jnp.concatenate([scale] * 3, axis=1)).astype(BF16)
            for n, v in enumerate((term, d * dot, d)):
                for q in range(3):
                    w = v[:, 128 * q : 128 * q + 128]
                    sums[n] = sums[n] + (w[:8] + w[8:])
            return tuple(sums)

        zero = jnp.zeros((8, 128), F32)
        sums = lax.fori_loop(0, 12, chunk, (zero, zero, zero))
        for n in range(3):
            acc[8 * n : 8 * n + 8, :] += sums[n]

    def image_grads(g):
        base = order[g] * (4 * ROWS)
        GI[rows_at(base, 4 * ROWS), :] = jnp.dot(PM[rows_at(base, 4 * ROWS), :], T[...], preferred_element_type=F32)

    def send_code(value, k, i, device, sem=None):
        encode(value, img_s.at[3 * k + i])
        return send(img_s.at[3 * k + i], img_r.at[3 * k + i], device, sem)

    def got(k, i):
        return decode(img_r.at[3 * k + i], SUB)

    def part(row, i):
        return GI.at[rows_at(row + i * SUB, SUB, SUB), :]

    messages, second = {}, {}

    def first_sends(g):
        base = order[g] * (4 * ROWS)
        for n, place in enumerate((2, 1, 3)):
            messages[3 * g + n] = [
                send_code(part(base + place * ROWS, i)[...], 3 * g + n, i, at_a(place)) for i in range(3)]

    def first_sum(g, i):
        value = part(order[g] * (4 * ROWS), i)[...]
        for k in range(3 * g, 3 * g + 3):
            messages[k][i].wait_recv()
            value = value + got(k, i)
        return value

    def close(g):
        k = 11 + order[g]
        if g == 0:
            second["sem"] = count[0]
            count[0] += 9
        second[g] = [
            send_code(first_sum(g, i), k, i, at_b(order[g]), second["sem"] + 3 * (order[g] - 1) + i) for i in range(3)]

    drained = [0, len(sent)]

    def drain():
        for copy in sent[drained[0] : drained[1]]:
            copy.wait_send()
        drained[:] = drained[1], len(sent)

    cores = {}

    def text_grads(g):
        n = len(GROUPS[g]) * ROWS
        base = text_row(GROUPS[g][0], 0)
        GT[pl.ds(base, 2 * n), :] = lax.dot_general(PM[:, base : base + 2 * n], I[...], (((0,), (0,)), ((), ())),
                                                    preferred_element_type=F32)
        for rel in GROUPS[g]:
            cores[rel] = send(GT.at[pl.ds(text_row(rel, 1), ROWS)], RT.at[pl.ds(rel * ROWS, ROWS)], at_core)

    def text_sum(rel, i):
        row = text_row(rel, 0) + i * SUB
        return GT[row : row + SUB, :] + RT[rel * ROWS + i * SUB : rel * ROWS + (i + 1) * SUB, :]

    zs = {}

    def z_send(k, rel, distance, incoming=()):
        zs[k] = []
        cores[rel].wait_recv()
        for i in range(3):
            value = text_sum(rel, i)
            for j in incoming:
                zs[j][i].wait_recv()
                value = value + decode(txt_r.at[3 * j + i], SUB)
            encode(value, txt_s.at[3 * k + i])
            zs[k].append(send(txt_s.at[3 * k + i], txt_r.at[3 * k + i], at_z(distance)))

    for g in range(4):
        pair(g, 0)
    text_grads(0)
    for g in range(4):
        pair(g, HALF)
        image_grads(g)
        first_sends(g)
        if g == 0:
            z_send(0, 4, 2)
            z_send(1, 3, 1)
            z_send(2, 5, 7)
            drain()
        elif g == 2:
            close(0)
    text_grads(1)
    sc_s[0] = acc[...]
    over_core = send(sc_s.at[0], sc_c, at_core)
    close(1)
    z_send(3, 6, 7, (2,))
    z_send(4, 2, 1, (1, 0))
    over_core.wait_recv()
    sc_s[1] = sc_s[0] + sc_c[...]
    sc_x[x] = sc_s[1]
    over_x = [send(sc_s.at[1], sc_x.at[x], at_x(d)) for d in (1, 2, 3)]
    close(2)
    text_grads(2)
    wait(over_x)
    sc_s[2] = (sc_x[0] + sc_x[1]) + (sc_x[2] + sc_x[3])
    sc_y[y] = sc_s[2]
    over_y = [send(sc_s.at[2], sc_y.at[y], at_y(d)) for d in (1, 2, 3)]
    drain()
    z_send(5, 7, 7, (3,))
    z_send(6, 1, 1, (4,))
    twin, side, across = [], [], []
    for i in range(3):
        value = first_sum(3, i)
        for g in range(3):
            second[g][i].wait_recv()
        for k in (12, 13, 14):
            value = value + got(k, i)
        twin.append(send_code(value, 15, i, at_y(dyt)))
        side.append(send(img_s.at[45 + i], img_r.at[48 + i], at_core))

    def image_out(row, i):
        return gimg_o.at[rows_at(row + i * SUB, SUB, SUB), :]

    for i in range(3):
        image_out(own_row, i)[...] = decode(img_s.at[45 + i], SUB)
    drain()
    wait(over_y)
    sc_s[3] = (sc_y[0] + sc_y[1]) + (sc_y[2] + sc_y[3])
    sc_z[z] = sc_s[3]
    over_z = [send(sc_s.at[3], sc_z.at[z], at_z(d)) for d in range(1, 8)]
    for i in range(3):
        side[i].wait_recv()
        image_out((lo * 2 + 1 - c) * ROWS, i)[...] = got(16, i)
    for i in range(3):
        twin[i].wait_recv()
        across.append(send(img_r.at[45 + i], img_r.at[51 + i], at_core))
        image_out(twin_row, i)[...] = got(15, i)
    for i in range(3):
        across[i].wait_recv()
        image_out(((1 - lo) * 2 + 1 - c) * ROWS, i)[...] = got(17, i)
    for i in range(3):
        if i == 0:
            cores[0].wait_recv()
        zs[5][i].wait_recv()
        zs[6][i].wait_recv()
        gtxt_o[i * SUB : i * SUB + SUB, :] = (
            text_sum(0, i) + decode(txt_r.at[15 + i], SUB) + decode(txt_r.at[18 + i], SUB))
    wait(over_z)
    total = sc_z[0]
    for i in range(1, 8):
        total = total + sc_z[i]
    pairs = 1.0 / (256.0 * ROWS * 256.0 * ROWS)
    loss_o[0] = -jnp.sum(total[0:8]) * pairs
    temp_o[0] = jnp.sum(total[8:16]) * pairs
    bias_o[0] = jnp.sum(total[16:24]) * pairs
    drain()
    drain()


def local(images, texts, log_temp, bias):
    sems = 200
    vmem = pl.BlockSpec(memory_space=pltpu.VMEM)
    smem = pl.BlockSpec(memory_space=pltpu.SMEM)
    hbm = pl.BlockSpec(memory_space=pltpu.HBM)
    scalar = jax.ShapeDtypeStruct((1,), F32)
    V = pltpu.VMEM
    return pl.pallas_call(
        kernel,
        out_shape=(scalar, jax.ShapeDtypeStruct((4 * ROWS, D), F32), jax.ShapeDtypeStruct((ROWS, D), F32), scalar, scalar),
        in_specs=[hbm, hbm, smem, smem],
        out_specs=(smem, vmem, vmem, smem, smem),
        scratch_shapes=[
            V((SIDE, D), BF16), V((SIDE, D), BF16), V((SIDE, SIDE), BF16), V((4 * ROWS, HALF), F32),
            V((SIDE, D), F32), V((SIDE, D), F32), V((SIDE // 2, D), F32),
            V((SIDE, 128), jnp.int32), V((8, SIDE), jnp.int32),
            V((48, 10, 16, 128), BF16), V((54, 10, 16, 128), BF16), V((21, 10, 16, 128), BF16), V((21, 10, 16, 128), BF16),
            V((4, 24, 128), F32), V((4, 24, 128), F32), V((4, 24, 128), F32), V((8, 24, 128), F32),
            V((24, 128), F32), V((24, 128), F32),
            pltpu.SemaphoreType.DMA((sems,)), pltpu.SemaphoreType.DMA((sems,)), pltpu.SemaphoreType.DMA((3,)),
        ],
        compiler_params=pltpu.CompilerParams(collective_id=0, has_side_effects=True, vmem_limit_bytes=48 << 20),
        name="pairs",
    )(images, texts, log_temp, bias)


def solution(mesh):
    return jax.shard_map(
        local,
        mesh=mesh,
        in_specs=(P("grp", None), P(("blk", "grp"), None), P(), P()),
        out_specs=(P(), P("grp", None), P(("blk", "grp"), None), P(), P()),
        check_vma=False,
    )
```

```python
import functools

import jax
import jax.numpy as jnp
from jax import lax
from jax.experimental import pallas as pl
from jax.experimental.pallas import tpu as pltpu
from jax.sharding import PartitionSpec as P

MESH = pl.DeviceIdType.MESH
F32 = jnp.float32
BF16 = jnp.bfloat16

ROWS = 48
D = 1152
NX, NY, NZ = 4, 4, 8
SIDE = 16 * ROWS
SUB = 16
HALF = SIDE // 2

GROUPS = ((4, 3, 5), (2, 6), (1, 7, 0))
LOW, HIGH = 2.0**-6, 2.0**6 - 2.0**-6


def text_row(rel, other):
    base = 0
    for group in GROUPS:
        if rel in group:
            return base + (other * len(group) + group.index(rel)) * ROWS
        base += 2 * len(group) * ROWS
    raise ValueError(rel)


def encode(value, message):
    tiles = [(r, j) for r in range(0, value.shape[0], 16) for j in range(0, D, 128)]
    top = jnp.full((16, 128), 1e-30, F32)
    for r, j in tiles:
        top = jnp.maximum(top, jnp.abs(value[r : r + 16, j : j + 128]))
    top = (top * 1.004).astype(BF16)
    gain = HIGH / top.astype(F32)
    for n, (r, j) in enumerate(tiles):
        v = value[r : r + 16, j : j + 128]
        t = jnp.abs(v) * gain + LOW
        for _ in range(4):
            t = t * t
        message[n] = jnp.where(v < 0, -t, t).astype(BF16)
    message[len(tiles)] = top


def decode(message, rows):
    count = rows // 16 * (D // 128)
    gain = message[count].astype(F32) * (1.0 / HIGH)
    out = []
    for n in range(count):
        v = message[n].astype(F32)
        t = (jnp.exp2(jnp.log2(jnp.abs(v)) * 0.0625) - LOW) * gain
        out.append(jnp.where(v < 0, -t, t))
    width = D // 128
    return jnp.concatenate(
        [jnp.concatenate(out[i : i + width], axis=1) for i in range(0, count, width)], axis=0)


def kernel(img, txt, lt, bs, loss_o, gimg_o, gtxt_o, temp_o, bias_o,
           I, T, PM, L, GI, GT, RT, rid, cid,
           img_s, img_r, txt_s, txt_r,
           sc_s, sc_x, sc_y, sc_z, sc_c, acc, ss, rs, ls):
    blk, grp = lax.axis_index("blk"), lax.axis_index("grp")
    lo, c = lax.div(blk, 2), lax.rem(blk, 2)
    h, z, x = lax.div(grp, 32), lax.rem(lax.div(grp, 4), 8), lax.rem(grp, 4)
    y = 2 * h + lo
    s = 1 - 2 * c

    def dev(x, y, z, c):
        return (lax.rem(y, 2) * 2 + c, lax.div(y, 2) * 32 + z * 4 + x)

    def at_x(d):
        return dev(lax.rem(x + d, 4), y, z, c)

    def at_y(d):
        return dev(x, lax.rem(y + d, 4), z, c)

    def at_z(d):
        return dev(x, y, lax.rem(z + s * d + 8, 8), c)

    def at_a(d):
        return dev(lax.rem(x + d * (1 - c), 4), lax.rem(y + d * c, 4), z, c)

    def at_b(d):
        return dev(lax.rem(x + d * c, 4), lax.rem(y + d * (1 - c), 4), z, c)

    at_core = dev(x, y, z, 1 - c)
    dyt, dyf = 1 + 2 * lo, 3 - 2 * lo

    barrier = pltpu.get_barrier_semaphore()
    peers = [at_x(1), at_x(2), at_x(3), at_y(1), at_y(2), at_y(3)] + [at_z(d) for d in range(1, 8)]
    peers += [at_core]
    for peer in peers:
        pl.semaphore_signal(barrier, inc=1, device_id=peer, device_id_type=MESH)

    def slot(dx, dy):
        return (dx * (1 + 3 * c) + dy * (4 - 3 * c)) * ROWS

    def rows_at(start, n, unit=ROWS):
        return pl.ds(pl.multiple_of(start, unit), n)

    mine = []
    for k, (dy, q) in enumerate(((0, lo), (dyt, 1 - lo))):
        mine.append(pltpu.make_async_copy(
            img.at[rows_at((q * 2 + c) * ROWS, ROWS)], I.at[rows_at(slot(0, dy), ROWS)], ls.at[k]))
    mine.append(pltpu.make_async_copy(txt, T.at[pl.ds(text_row(0, 0), ROWS)], ls.at[2]))
    for copy in mine:
        copy.start()

    for dy in range(4):
        for dx in range(4):
            x2, y2 = lax.rem(x + dx, 4), lax.rem(y + dy, 4)
            first = (lax.div(y2, 2) * 32 + z * 4 + x2) * 192 + (lax.rem(y2, 2) * 2 + c) * ROWS
            rid[rows_at(slot(dx, dy), ROWS), :] = first + lax.broadcasted_iota(jnp.int32, (ROWS, 128), 0)
    lane = lax.broadcasted_iota(jnp.int32, (8, SIDE), 1)
    ids = jnp.zeros((8, SIDE), jnp.int32)
    for rel in range(8):
        for other in range(2):
            z2 = lax.rem(z + (s if other == 0 else -s) * rel + 8, 8)
            c2 = c if other == 0 else 1 - c
            row = text_row(rel, other)
            first = (lo * 2 + c2) * 3072 + (h * 32 + z2 * 4 + x) * ROWS - row
            ids = jnp.where((lane >= row) & (lane < row + ROWS), lane + first, ids)
    cid[...] = ids
    acc[...] = jnp.zeros_like(acc)
    scale = jnp.exp(jnp.full((1, 128), lt[0], F32))
    shift = bs[0]

    pl.semaphore_wait(barrier, len(peers))

    sent = []
    count = [0]

    def send(src, dst, device, sem=None):
        k = count[0] if sem is None else sem
        if sem is None:
            count[0] += 1
        copy = pltpu.make_async_remote_copy(
            src_ref=src, dst_ref=dst, send_sem=ss.at[k], recv_sem=rs.at[k], device_id=device, device_id_type=MESH)
        copy.start()
        sent.append(copy)
        return copy

    def send_piece(src, src_row, dst, dst_row, device, subs=3):
        n = ROWS // subs
        return [send(src.at[rows_at(src_row + i * n, n, n)], dst.at[rows_at(dst_row + i * n, n, n)], device)
                for i in range(subs)]

    def wait(copies):
        for copy in copies:
            copy.wait_recv()

    own_row, twin_row = (lo * 2 + c) * ROWS, ((1 - lo) * 2 + c) * ROWS
    dxs, dxi = 1 + 2 * lo, 3 - 2 * lo

    def hop(src, src_row, dst, dst_row, i, device):
        return send(src.at[rows_at(src_row + i * SUB, SUB, SUB)], dst.at[rows_at(dst_row + i * SUB, SUB, SUB)], device)

    def text_hop(rel, into, i, distance):
        return hop(T, text_row(rel, 0), T, text_row(into, 0), i, at_z(distance))

    t7, t1, t6, t2, t5, t4, t3 = [], [], [], [], [], [], []
    xp0, xm1, xp1, xm0, yf0 = [], [], [], [], []
    for i in range(3):
        t7.append(hop(txt, 0, T, text_row(7, 0), i, at_z(1)))
        t1.append(hop(txt, 0, T, text_row(1, 0), i, at_z(7)))
        xp0.append(hop(img, own_row, I, slot(3, 0), i, at_x(1)))
        xm1.append(hop(img, twin_row, I, slot(1, dyt), i, at_x(3)))
        yf0.append(hop(img, own_row, I, slot(0, dyt), i, at_y(dyf)))
    for i in range(3):
        xp1.append(hop(img, twin_row, I, slot(3, dyt), i, at_x(1)))
        xm0.append(hop(img, own_row, I, slot(1, 0), i, at_x(3)))
    t_c = [send_piece(txt, 0, T, text_row(0, 1), at_core, 1)]

    xpf, xmf, y1, y2, w0, w1, w2, v1, v2 = [], [], [], [], [], [], [], [], []
    for i in range(3):
        t7[i].wait_recv()
        t6.append(text_hop(7, 6, i, 1))
        t1[i].wait_recv()
        t2.append(text_hop(1, 2, i, 7))
        xp0[i].wait_recv()
        xm1[i].wait_recv()
        y1.append(hop(I, slot(dxs, 1 - lo), I, slot(dxs, 2 + lo), i, at_y(dyf)))
        xpf.append(hop(I, slot(3, 0), I, slot(2, 0), i, at_x(1)))
        xmf.append(hop(I, slot(1, dyt), I, slot(2, dyt), i, at_x(3)))
        yf0[i].wait_recv()
        w0.append(hop(I, slot(0, dyf), I, slot(0, 2), i, at_y(dyt)))
    t_c.append(send_piece(T, text_row(7, 0), T, text_row(7, 1), at_core, 1))
    t_c.append(send_piece(T, text_row(1, 0), T, text_row(1, 1), at_core, 1))
    for i in range(3):
        xp1[i].wait_recv()
        xm0[i].wait_recv()
        y2.append(hop(I, slot(dxs, 3 * lo), I, slot(dxs, 1 + lo), i, at_y(dyf)))
    for i in range(3):
        y1[i].wait_recv()
        w1.append(hop(I, slot(dxi, 3 - lo), I, slot(dxi, 2 + lo), i, at_y(dyt)))
        v1.append(hop(I, slot(dxi, 3 - lo), I, slot(2, 3 - lo), i, at_x(dxs)))
        t6[i].wait_recv()
        t5.append(text_hop(6, 5, i, 1))
        t4.append(text_hop(6, 4, i, 2))
        t2[i].wait_recv()
        t3.append(text_hop(2, 3, i, 7))
    t_c.append(send_piece(T, text_row(6, 0), T, text_row(6, 1), at_core, 1))
    t_c.append(send_piece(T, text_row(2, 0), T, text_row(2, 1), at_core, 1))
    for i in range(3):
        y2[i].wait_recv()
        w2.append(hop(I, slot(dxi, 2 - lo), I, slot(dxi, 1 + lo), i, at_y(dyt)))
        v2.append(hop(I, slot(dxi, 2 - lo), I, slot(2, 2 - lo), i, at_x(dxs)))
    for i in range(3):
        for rel, copies in ((3, t3), (5, t5)):
            copies[i].wait_recv()
            t_c.append([hop(T, text_row(rel, 0), T, text_row(rel, 1), i, at_core)])
    for i in range(3):
        t4[i].wait_recv()
        t_c.append([hop(T, text_row(4, 0), T, text_row(4, 1), i, at_core)])

    g1 = (1 + 2 * lo) * (1 - c) + c
    order = (2, g1, 4 - g1, 0)

    def pair(g, j):
        base = order[g] * (4 * ROWS)
        L[...] = lax.dot_general(I[rows_at(base, 4 * ROWS), :], T[j : j + HALF, :], (((1,), (1,)), ((), ())),
                                 preferred_element_type=F32)

        def chunk(i, carry):
            r = pl.multiple_of(i * 16, 16)
            rg = pl.multiple_of(base + i * 16, 16)
            rows = rid[pl.ds(rg, 16), :]
            sums = list(carry)
            dot = L[pl.ds(r, 16), :] * jnp.concatenate([scale] * 3, axis=1)
            same = jnp.concatenate([rows] * 3, axis=1) == jnp.concatenate([cid[:, j : j + HALF]] * 2, axis=0)
            logit = dot + shift
            signed = jnp.where(same, logit, -logit)
            e = jnp.exp(-jnp.abs(signed))
            inv = 1.0 / (1.0 + e)
            term = jnp.minimum(signed, 0.0) - jnp.log1p(e)
            d = jnp.where(signed >= 0, e, 1.0) * inv
            d = jnp.where(same, -d, d)
            PM[pl.ds(rg, 16), j : j + HALF] = (d * jnp.concatenate([scale] * 3, axis=1)).astype(BF16)
            for n, v in enumerate((term, d * dot, d)):
                for q in range(3):
                    w = v[:, 128 * q : 128 * q + 128]
                    sums[n] = sums[n] + (w[:8] + w[8:])
            return tuple(sums)

        zero = jnp.zeros((8, 128), F32)
        sums = lax.fori_loop(0, 12, chunk, (zero, zero, zero))
        for n in range(3):
            acc[8 * n : 8 * n + 8, :] += sums[n]

    def image_grads(g):
        base = order[g] * (4 * ROWS)
        GI[rows_at(base, 4 * ROWS), :] = jnp.dot(PM[rows_at(base, 4 * ROWS), :], T[...], preferred_element_type=F32)

    def send_code(value, k, i, device, sem=None):
        encode(value, img_s.at[3 * k + i])
        return send(img_s.at[3 * k + i], img_r.at[3 * k + i], device, sem)

    def got(k, i):
        return decode(img_r.at[3 * k + i], SUB)

    def part(row, i):
        return GI.at[rows_at(row + i * SUB, SUB, SUB), :]

    messages, second = {}, {}

    def first_sends(g):
        base = order[g] * (4 * ROWS)
        for n, place in enumerate((2, 1, 3)):
            messages[3 * g + n] = [
                send_code(part(base + place * ROWS, i)[...], 3 * g + n, i, at_a(place)) for i in range(3)]

    def first_sum(g, i):
        value = part(order[g] * (4 * ROWS), i)[...]
        for k in range(3 * g, 3 * g + 3):
            messages[k][i].wait_recv()
            value = value + got(k, i)
        return value

    def close(g):
        k = 11 + order[g]
        if g == 0:
            second["sem"] = count[0]
            count[0] += 9
        second[g] = [
            send_code(first_sum(g, i), k, i, at_b(order[g]), second["sem"] + 3 * (order[g] - 1) + i) for i in range(3)]

    drained = [0, len(sent)]

    def drain():
        for copy in sent[drained[0] : drained[1]]:
            copy.wait_send()
        drained[:] = drained[1], len(sent)

    cores = {}

    def text_grads(g):
        n = len(GROUPS[g]) * ROWS
        base = text_row(GROUPS[g][0], 0)
        GT[pl.ds(base, 2 * n), :] = lax.dot_general(PM[:, base : base + 2 * n], I[...], (((0,), (0,)), ((), ())),
                                                    preferred_element_type=F32)
        for rel in GROUPS[g]:
            cores[rel] = send(GT.at[pl.ds(text_row(rel, 1), ROWS)], RT.at[pl.ds(rel * ROWS, ROWS)], at_core)

    def text_sum(rel, i):
        row = text_row(rel, 0) + i * SUB
        return GT[row : row + SUB, :] + RT[rel * ROWS + i * SUB : rel * ROWS + (i + 1) * SUB, :]

    zs = {}

    def z_send(k, rel, distance, incoming=()):
        zs[k] = []
        cores[rel].wait_recv()
        for i in range(3):
            value = text_sum(rel, i)
            for j in incoming:
                zs[j][i].wait_recv()
                value = value + decode(txt_r.at[3 * j + i], SUB)
            encode(value, txt_s.at[3 * k + i])
            zs[k].append(send(txt_s.at[3 * k + i], txt_r.at[3 * k + i], at_z(distance)))

    for copies in t_c[:5]:
        wait(copies)
    for copy in mine:
        copy.wait()
    for copies in (xpf, xmf, w0):
        wait(copies)
    pair(3, HALF)
    for copies in t_c[5:]:
        wait(copies)
    for copies in (w1, w2, v1, v2):
        wait(copies)
    for g in (0, 1):
        pair(g, 0)
        pair(g, HALF)
        image_grads(g)
        first_sends(g)
    pair(2, 0)
    pair(3, 0)
    text_grads(0)
    pair(2, HALF)
    sc_s[0] = acc[...]
    sc_x[x] = sc_s[0]
    over_x = [send(sc_s.at[0], sc_x.at[x], at_x(d)) for d in (1, 2, 3)]
    image_grads(2)
    first_sends(2)
    z_send(0, 4, 2)
    z_send(1, 3, 1)
    z_send(2, 5, 7)
    image_grads(3)
    first_sends(3)
    close(0)
    text_grads(1)
    wait(over_x)
    sc_s[1] = (sc_x[0] + sc_x[1]) + (sc_x[2] + sc_x[3])
    sc_y[y] = sc_s[1]
    over_y = [send(sc_s.at[1], sc_y.at[y], at_y(d)) for d in (1, 2, 3)]
    drain()
    close(1)
    z_send(3, 6, 7, (2,))
    z_send(4, 2, 1, (1, 0))
    close(2)
    wait(over_y)
    sc_s[2] = (sc_y[0] + sc_y[1]) + (sc_y[2] + sc_y[3])
    sc_z[z] = sc_s[2]
    over_z = [send(sc_s.at[2], sc_z.at[z], at_z(d)) for d in range(1, 8)]
    text_grads(2)
    drain()
    twin, side, across = [], [], []
    for i in range(3):
        value = first_sum(3, i)
        for g in range(3):
            second[g][i].wait_recv()
        for k in (12, 13, 14):
            value = value + got(k, i)
        twin.append(send_code(value, 15, i, at_y(dyt)))
        side.append(send(img_s.at[45 + i], img_r.at[48 + i], at_core))
    z_send(5, 7, 7, (3,))
    z_send(6, 1, 1, (4,))

    wait(over_z)
    total = sc_z[0]
    for i in range(1, 8):
        total = total + sc_z[i]
    sc_s[3] = total
    over_core = send(sc_s.at[3], sc_c, at_core)

    def image_out(row, i):
        return gimg_o.at[rows_at(row + i * SUB, SUB, SUB), :]

    drain()
    for i in range(3):
        image_out(own_row, i)[...] = decode(img_s.at[45 + i], SUB)
    for i in range(3):
        side[i].wait_recv()
        image_out((lo * 2 + 1 - c) * ROWS, i)[...] = got(16, i)
    over_core.wait_recv()
    total = sc_s[3] + sc_c[...]
    pairs = 1.0 / (256.0 * ROWS * 256.0 * ROWS)
    loss_o[0] = -jnp.sum(total[0:8]) * pairs
    temp_o[0] = jnp.sum(total[8:16]) * pairs
    bias_o[0] = jnp.sum(total[16:24]) * pairs
    for i in range(3):
        twin[i].wait_recv()
        across.append(send(img_r.at[45 + i], img_r.at[51 + i], at_core))
        image_out(twin_row, i)[...] = got(15, i)
    for i in range(3):
        if i == 0:
            cores[0].wait_recv()
        zs[5][i].wait_recv()
        zs[6][i].wait_recv()
        gtxt_o[i * SUB : i * SUB + SUB, :] = (
            text_sum(0, i) + decode(txt_r.at[15 + i], SUB) + decode(txt_r.at[18 + i], SUB))
    drain()
    for i in range(3):
        across[i].wait_recv()
        image_out(((1 - lo) * 2 + 1 - c) * ROWS, i)[...] = got(17, i)
    drain()
    drain()


def local(images, texts, log_temp, bias):
    sems = 200
    vmem = pl.BlockSpec(memory_space=pltpu.VMEM)
    smem = pl.BlockSpec(memory_space=pltpu.SMEM)
    hbm = pl.BlockSpec(memory_space=pltpu.HBM)
    scalar = jax.ShapeDtypeStruct((1,), F32)
    V = pltpu.VMEM
    return pl.pallas_call(
        kernel,
        out_shape=(scalar, jax.ShapeDtypeStruct((4 * ROWS, D), F32), jax.ShapeDtypeStruct((ROWS, D), F32), scalar, scalar),
        in_specs=[hbm, hbm, smem, smem],
        out_specs=(smem, vmem, vmem, smem, smem),
        scratch_shapes=[
            V((SIDE, D), BF16), V((SIDE, D), BF16), V((SIDE, SIDE), BF16), V((4 * ROWS, HALF), F32),
            V((SIDE, D), F32), V((SIDE, D), F32), V((SIDE // 2, D), F32),
            V((SIDE, 128), jnp.int32), V((8, SIDE), jnp.int32),
            V((48, 10, 16, 128), BF16), V((54, 10, 16, 128), BF16), V((21, 10, 16, 128), BF16), V((21, 10, 16, 128), BF16),
            V((4, 24, 128), F32), V((4, 24, 128), F32), V((4, 24, 128), F32), V((8, 24, 128), F32),
            V((24, 128), F32), V((24, 128), F32),
            pltpu.SemaphoreType.DMA((sems,)), pltpu.SemaphoreType.DMA((sems,)), pltpu.SemaphoreType.DMA((3,)),
        ],
        compiler_params=pltpu.CompilerParams(collective_id=0, has_side_effects=True, vmem_limit_bytes=48 << 20),
        name="pairs",
    )(images, texts, log_temp, bias)


def solution(mesh):
    return jax.shard_map(
        local,
        mesh=mesh,
        in_specs=(P("grp", None), P(("blk", "grp"), None), P(), P()),
        out_specs=(P(), P("grp", None), P(("blk", "grp"), None), P(), P()),
        check_vma=False,
    )
```

```python
import functools

import jax
import jax.numpy as jnp
from jax import lax
from jax.experimental import pallas as pl
from jax.experimental.pallas import tpu as pltpu
from jax.sharding import PartitionSpec as P

MESH = pl.DeviceIdType.MESH
F32 = jnp.float32
BF16 = jnp.bfloat16

ROWS = 48
D = 1152
NX, NY, NZ = 4, 4, 8
SIDE = 16 * ROWS
SUB = 16
HALF = SIDE // 2

GROUPS = ((4, 3, 5), (2, 6), (1, 7, 0))
LOW, HIGH = 2.0**-6, 2.0**6 - 2.0**-6


def text_row(rel, other):
    base = 0
    for group in GROUPS:
        if rel in group:
            return base + (other * len(group) + group.index(rel)) * ROWS
        base += 2 * len(group) * ROWS
    raise ValueError(rel)


def encode(value, message):
    tiles = [(r, j) for r in range(0, value.shape[0], 16) for j in range(0, D, 128)]
    top = jnp.full((16, 128), 1e-30, F32)
    for r, j in tiles:
        top = jnp.maximum(top, jnp.abs(value[r : r + 16, j : j + 128]))
    top = (top * 1.004).astype(BF16)
    gain = HIGH / top.astype(F32)
    for n, (r, j) in enumerate(tiles):
        v = value[r : r + 16, j : j + 128]
        t = jnp.abs(v) * gain + LOW
        for _ in range(4):
            t = t * t
        message[n] = jnp.where(v < 0, -t, t).astype(BF16)
    message[len(tiles)] = top


def decode(message, rows):
    count = rows // 16 * (D // 128)
    gain = message[count].astype(F32) * (1.0 / HIGH)
    out = []
    for n in range(count):
        v = message[n].astype(F32)
        t = (jnp.exp2(jnp.log2(jnp.abs(v)) * 0.0625) - LOW) * gain
        out.append(jnp.where(v < 0, -t, t))
    width = D // 128
    return jnp.concatenate(
        [jnp.concatenate(out[i : i + width], axis=1) for i in range(0, count, width)], axis=0)


def kernel(img, txt, lt, bs, loss_o, gimg_o, gtxt_o, temp_o, bias_o,
           I, T, PM, L, GI, GT, RT, rid, cid,
           img_s, img_r, txt_s, txt_r,
           sc_s, sc_x, sc_y, sc_z, sc_c, acc, ss, rs, ls):
    blk, grp = lax.axis_index("blk"), lax.axis_index("grp")
    lo, c = lax.div(blk, 2), lax.rem(blk, 2)
    h, z, x = lax.div(grp, 32), lax.rem(lax.div(grp, 4), 8), lax.rem(grp, 4)
    y = 2 * h + lo
    s = 1 - 2 * c

    def dev(x, y, z, c):
        return (lax.rem(y, 2) * 2 + c, lax.div(y, 2) * 32 + z * 4 + x)

    def at_x(d):
        return dev(lax.rem(x + d, 4), y, z, c)

    def at_y(d):
        return dev(x, lax.rem(y + d, 4), z, c)

    def at_z(d):
        return dev(x, y, lax.rem(z + s * d + 8, 8), c)

    def at_a(d):
        return dev(lax.rem(x + d * (1 - c), 4), lax.rem(y + d * c, 4), z, c)

    def at_b(d):
        return dev(lax.rem(x + d * c, 4), lax.rem(y + d * (1 - c), 4), z, c)

    at_core = dev(x, y, z, 1 - c)
    dyt, dyf = 1 + 2 * lo, 3 - 2 * lo

    barrier = pltpu.get_barrier_semaphore()
    peers = [at_x(1), at_x(2), at_x(3), at_y(1), at_y(2), at_y(3)] + [at_z(d) for d in range(1, 8)]
    peers += [at_core]
    for peer in peers:
        pl.semaphore_signal(barrier, inc=1, device_id=peer, device_id_type=MESH)

    def slot(dx, dy):
        return (dx * (1 + 3 * c) + dy * (4 - 3 * c)) * ROWS

    def rows_at(start, n, unit=ROWS):
        return pl.ds(pl.multiple_of(start, unit), n)

    mine = []
    for k, (dy, q) in enumerate(((0, lo), (dyt, 1 - lo))):
        mine.append(pltpu.make_async_copy(
            img.at[rows_at((q * 2 + c) * ROWS, ROWS)], I.at[rows_at(slot(0, dy), ROWS)], ls.at[k]))
    mine.append(pltpu.make_async_copy(txt, T.at[pl.ds(text_row(0, 0), ROWS)], ls.at[2]))
    for copy in mine:
        copy.start()

    for dy in range(4):
        for dx in range(4):
            x2, y2 = lax.rem(x + dx, 4), lax.rem(y + dy, 4)
            first = (lax.div(y2, 2) * 32 + z * 4 + x2) * 192 + (lax.rem(y2, 2) * 2 + c) * ROWS
            rid[rows_at(slot(dx, dy), ROWS), :] = first + lax.broadcasted_iota(jnp.int32, (ROWS, 128), 0)
    lane = lax.broadcasted_iota(jnp.int32, (8, SIDE), 1)
    ids = jnp.zeros((8, SIDE), jnp.int32)
    for rel in range(8):
        for other in range(2):
            z2 = lax.rem(z + (s if other == 0 else -s) * rel + 8, 8)
            c2 = c if other == 0 else 1 - c
            row = text_row(rel, other)
            first = (lo * 2 + c2) * 3072 + (h * 32 + z2 * 4 + x) * ROWS - row
            ids = jnp.where((lane >= row) & (lane < row + ROWS), lane + first, ids)
    cid[...] = ids
    acc[...] = jnp.zeros_like(acc)
    scale = jnp.exp(jnp.full((1, 128), lt[0], F32))
    shift = bs[0]

    pl.semaphore_wait(barrier, len(peers))

    sent = []
    count = [0]

    def send(src, dst, device, sem=None):
        k = count[0] if sem is None else sem
        if sem is None:
            count[0] += 1
        copy = pltpu.make_async_remote_copy(
            src_ref=src, dst_ref=dst, send_sem=ss.at[k], recv_sem=rs.at[k], device_id=device, device_id_type=MESH)
        copy.start()
        sent.append(copy)
        return copy

    def send_piece(src, src_row, dst, dst_row, device, subs=3):
        n = ROWS // subs
        return [send(src.at[rows_at(src_row + i * n, n, n)], dst.at[rows_at(dst_row + i * n, n, n)], device)
                for i in range(subs)]

    def wait(copies):
        for copy in copies:
            copy.wait_recv()

    own_row, twin_row = (lo * 2 + c) * ROWS, ((1 - lo) * 2 + c) * ROWS
    dxs, dxi = 1 + 2 * lo, 3 - 2 * lo

    def hop(src, src_row, dst, dst_row, i, device):
        return send(src.at[rows_at(src_row + i * SUB, SUB, SUB)], dst.at[rows_at(dst_row + i * SUB, SUB, SUB)], device)

    def text_hop(rel, into, i, distance):
        return hop(T, text_row(rel, 0), T, text_row(into, 0), i, at_z(distance))

    t7, t1, t6, t2, t5, t4, t3 = [], [], [], [], [], [], []
    xp0, xm1, xp1, xm0, yf0 = [], [], [], [], []
    for i in range(3):
        t7.append(hop(txt, 0, T, text_row(7, 0), i, at_z(1)))
        t1.append(hop(txt, 0, T, text_row(1, 0), i, at_z(7)))
        xp0.append(hop(img, own_row, I, slot(3, 0), i, at_x(1)))
        xm1.append(hop(img, twin_row, I, slot(1, dyt), i, at_x(3)))
        yf0.append(hop(img, own_row, I, slot(0, dyt), i, at_y(dyf)))
    for i in range(3):
        xp1.append(hop(img, twin_row, I, slot(3, dyt), i, at_x(1)))
        xm0.append(hop(img, own_row, I, slot(1, 0), i, at_x(3)))
    t_c = [send_piece(txt, 0, T, text_row(0, 1), at_core, 1)]

    xpf, xmf, y1, y2, w0, w1, w2, v1, v2 = [], [], [], [], [], [], [], [], []
    for i in range(3):
        t7[i].wait_recv()
        t6.append(text_hop(7, 6, i, 1))
        t1[i].wait_recv()
        t2.append(text_hop(1, 2, i, 7))
        xp0[i].wait_recv()
        xm1[i].wait_recv()
        y1.append(hop(I, slot(dxs, 1 - lo), I, slot(dxs, 2 + lo), i, at_y(dyf)))
        xpf.append(hop(I, slot(3, 0), I, slot(2, 0), i, at_x(1)))
        xmf.append(hop(I, slot(1, dyt), I, slot(2, dyt), i, at_x(3)))
        yf0[i].wait_recv()
        w0.append(hop(I, slot(0, dyf), I, slot(0, 2), i, at_y(dyt)))
    t_c.append(send_piece(T, text_row(7, 0), T, text_row(7, 1), at_core, 1))
    t_c.append(send_piece(T, text_row(1, 0), T, text_row(1, 1), at_core, 1))
    for i in range(3):
        xp1[i].wait_recv()
        xm0[i].wait_recv()
        y2.append(hop(I, slot(dxs, 3 * lo), I, slot(dxs, 1 + lo), i, at_y(dyf)))
    for i in range(3):
        y1[i].wait_recv()
        w1.append(hop(I, slot(dxi, 3 - lo), I, slot(dxi, 2 + lo), i, at_y(dyt)))
        v1.append(hop(I, slot(dxi, 3 - lo), I, slot(2, 3 - lo), i, at_x(dxs)))
        t6[i].wait_recv()
        t5.append(text_hop(6, 5, i, 1))
        t4.append(text_hop(6, 4, i, 2))
        t2[i].wait_recv()
        t3.append(text_hop(2, 3, i, 7))
    t_c.append(send_piece(T, text_row(6, 0), T, text_row(6, 1), at_core, 1))
    t_c.append(send_piece(T, text_row(2, 0), T, text_row(2, 1), at_core, 1))
    for i in range(3):
        y2[i].wait_recv()
        w2.append(hop(I, slot(dxi, 2 - lo), I, slot(dxi, 1 + lo), i, at_y(dyt)))
        v2.append(hop(I, slot(dxi, 2 - lo), I, slot(2, 2 - lo), i, at_x(dxs)))
    for i in range(3):
        for rel, copies in ((3, t3), (5, t5)):
            copies[i].wait_recv()
            t_c.append([hop(T, text_row(rel, 0), T, text_row(rel, 1), i, at_core)])
    for i in range(3):
        t4[i].wait_recv()
        t_c.append([hop(T, text_row(4, 0), T, text_row(4, 1), i, at_core)])

    g1 = (1 + 2 * lo) * (1 - c) + c
    order = (2, g1, 4 - g1, 0)

    def pair(g, j):
        base = order[g] * (4 * ROWS)
        L[...] = lax.dot_general(I[rows_at(base, 4 * ROWS), :], T[j : j + HALF, :], (((1,), (1,)), ((), ())),
                                 preferred_element_type=F32)

        def chunk(i, carry):
            r = pl.multiple_of(i * 16, 16)
            rg = pl.multiple_of(base + i * 16, 16)
            rows = rid[pl.ds(rg, 16), :]
            sums = list(carry)
            dot = L[pl.ds(r, 16), :] * jnp.concatenate([scale] * 3, axis=1)
            same = jnp.concatenate([rows] * 3, axis=1) == jnp.concatenate([cid[:, j : j + HALF]] * 2, axis=0)
            logit = dot + shift
            signed = jnp.where(same, logit, -logit)
            e = jnp.exp(-jnp.abs(signed))
            inv = 1.0 / (1.0 + e)
            term = jnp.minimum(signed, 0.0) - jnp.log1p(e)
            d = jnp.where(signed >= 0, e, 1.0) * inv
            d = jnp.where(same, -d, d)
            PM[pl.ds(rg, 16), j : j + HALF] = (d * jnp.concatenate([scale] * 3, axis=1)).astype(BF16)
            for n, v in enumerate((term, d * dot, d)):
                for q in range(3):
                    w = v[:, 128 * q : 128 * q + 128]
                    sums[n] = sums[n] + (w[:8] + w[8:])
            return tuple(sums)

        zero = jnp.zeros((8, 128), F32)
        sums = lax.fori_loop(0, 12, chunk, (zero, zero, zero))
        for n in range(3):
            acc[8 * n : 8 * n + 8, :] += sums[n]

    def image_grads(g):
        base = order[g] * (4 * ROWS)
        GI[rows_at(base, 4 * ROWS), :] = jnp.dot(PM[rows_at(base, 4 * ROWS), :], T[...], preferred_element_type=F32)

    def box(ref, n, tiles=10):
        return ref.at[pl.ds(n * 10, tiles)]

    def send_code(value, k, i, device, sem=None):
        encode(value, box(img_s, 3 * k + i))
        return send(box(img_s, 3 * k + i), box(img_r, 3 * k + i), device, sem)

    def got(k, i):
        return decode(box(img_r, 3 * k + i), SUB)

    def part(row, i):
        return GI.at[rows_at(row + i * SUB, SUB, SUB), :]

    messages, second = {}, {}

    def first_sends(g):
        base = order[g] * (4 * ROWS)
        for n, place in enumerate((2, 1, 3)):
            k = 3 * g + n
            if g < 3:
                encode(GI[rows_at(base + place * ROWS, ROWS), :], box(img_s, 3 * k, 28))
                messages[k] = send(box(img_s, 3 * k, 28), box(img_r, 3 * k, 28), at_a(place))
                continue
            messages[k] = [
                send_code(part(base + place * ROWS, i)[...], 3 * g + n, i, at_a(place)) for i in range(3)]

    def first_sum(g, i):
        value = part(order[g] * (4 * ROWS), i)[...]
        for k in range(3 * g, 3 * g + 3):
            messages[k][i].wait_recv()
            value = value + got(k, i)
        return value

    def close(g):
        k = 11 + order[g]
        if g == 0:
            second["sem"] = count[0]
            count[0] += 9
        total = GI[rows_at(order[g] * (4 * ROWS), ROWS), :]
        for n in range(3 * g, 3 * g + 3):
            messages[n].wait_recv()
            total = total + decode(box(img_r, 3 * n, 28), ROWS)
        second[g] = [
            send_code(total[i * SUB : (i + 1) * SUB], k, i, at_b(order[g]), second["sem"] + 3 * (order[g] - 1) + i) for i in range(3)]

    drained = [0, len(sent)]

    def drain():
        for copy in sent[drained[0] : drained[1]]:
            copy.wait_send()
        drained[:] = drained[1], len(sent)

    cores = {}

    def text_grads(g):
        n = len(GROUPS[g]) * ROWS
        base = text_row(GROUPS[g][0], 0)
        GT[pl.ds(base, 2 * n), :] = lax.dot_general(PM[:, base : base + 2 * n], I[...], (((0,), (0,)), ((), ())),
                                                    preferred_element_type=F32)
        for rel in GROUPS[g]:
            cores[rel] = send(GT.at[pl.ds(text_row(rel, 1), ROWS)], RT.at[pl.ds(rel * ROWS, ROWS)], at_core)

    def text_sum(rel, i):
        row = text_row(rel, 0) + i * SUB
        return GT[row : row + SUB, :] + RT[rel * ROWS + i * SUB : rel * ROWS + (i + 1) * SUB, :]

    zs = {}

    def z_send(k, rel, distance, incoming=()):
        zs[k] = []
        cores[rel].wait_recv()
        for i in range(3):
            value = text_sum(rel, i)
            for j in incoming:
                zs[j][i].wait_recv()
                value = value + decode(txt_r.at[3 * j + i], SUB)
            encode(value, txt_s.at[3 * k + i])
            zs[k].append(send(txt_s.at[3 * k + i], txt_r.at[3 * k + i], at_z(distance)))

    for copies in t_c[:5]:
        wait(copies)
    for copy in mine:
        copy.wait()
    for copies in (xpf, xmf, w0):
        wait(copies)
    pair(3, HALF)
    for copies in t_c[5:]:
        wait(copies)
    for copies in (w1, w2, v1, v2):
        wait(copies)
    for g in (0, 1):
        pair(g, 0)
        pair(g, HALF)
        image_grads(g)
        first_sends(g)
    pair(2, 0)
    pair(3, 0)
    text_grads(0)
    pair(2, HALF)
    sc_s[0] = acc[...]
    sc_x[x] = sc_s[0]
    over_x = [send(sc_s.at[0], sc_x.at[x], at_x(d)) for d in (1, 2, 3)]
    image_grads(2)
    first_sends(2)
    z_send(0, 4, 2)
    z_send(1, 3, 1)
    z_send(2, 5, 7)
    image_grads(3)
    first_sends(3)
    close(0)
    text_grads(1)
    wait(over_x)
    sc_s[1] = (sc_x[0] + sc_x[1]) + (sc_x[2] + sc_x[3])
    sc_y[y] = sc_s[1]
    over_y = [send(sc_s.at[1], sc_y.at[y], at_y(d)) for d in (1, 2, 3)]
    drain()
    close(1)
    z_send(3, 6, 7, (2,))
    z_send(4, 2, 1, (1, 0))
    close(2)
    wait(over_y)
    sc_s[2] = (sc_y[0] + sc_y[1]) + (sc_y[2] + sc_y[3])
    sc_z[z] = sc_s[2]
    over_z = [send(sc_s.at[2], sc_z.at[z], at_z(d)) for d in range(1, 8)]
    text_grads(2)
    drain()
    twin, side, across = [], [], []
    for i in range(3):
        value = first_sum(3, i)
        for g in range(3):
            second[g][i].wait_recv()
        for k in (12, 13, 14):
            value = value + got(k, i)
        twin.append(send_code(value, 15, i, at_y(dyt)))
        side.append(send(box(img_s, 45 + i), box(img_r, 48 + i), at_core))
    z_send(5, 7, 7, (3,))
    z_send(6, 1, 1, (4,))

    wait(over_z)
    total = sc_z[0]
    for i in range(1, 8):
        total = total + sc_z[i]
    sc_s[3] = total
    over_core = send(sc_s.at[3], sc_c, at_core)

    def image_out(row, i):
        return gimg_o.at[rows_at(row + i * SUB, SUB, SUB), :]

    drain()
    for i in range(3):
        image_out(own_row, i)[...] = decode(box(img_s, 45 + i), SUB)
    for i in range(3):
        side[i].wait_recv()
        image_out((lo * 2 + 1 - c) * ROWS, i)[...] = got(16, i)
    over_core.wait_recv()
    total = sc_s[3] + sc_c[...]
    pairs = 1.0 / (256.0 * ROWS * 256.0 * ROWS)
    loss_o[0] = -jnp.sum(total[0:8]) * pairs
    temp_o[0] = jnp.sum(total[8:16]) * pairs
    bias_o[0] = jnp.sum(total[16:24]) * pairs
    for i in range(3):
        twin[i].wait_recv()
        across.append(send(box(img_r, 45 + i), box(img_r, 51 + i), at_core))
        image_out(twin_row, i)[...] = got(15, i)
    for i in range(3):
        if i == 0:
            cores[0].wait_recv()
        zs[5][i].wait_recv()
        zs[6][i].wait_recv()
        gtxt_o[i * SUB : i * SUB + SUB, :] = (
            text_sum(0, i) + decode(txt_r.at[15 + i], SUB) + decode(txt_r.at[18 + i], SUB))
    drain()
    for i in range(3):
        across[i].wait_recv()
        image_out(((1 - lo) * 2 + 1 - c) * ROWS, i)[...] = got(17, i)
    drain()
    drain()


def local(images, texts, log_temp, bias):
    sems = 200
    vmem = pl.BlockSpec(memory_space=pltpu.VMEM)
    smem = pl.BlockSpec(memory_space=pltpu.SMEM)
    hbm = pl.BlockSpec(memory_space=pltpu.HBM)
    scalar = jax.ShapeDtypeStruct((1,), F32)
    V = pltpu.VMEM
    return pl.pallas_call(
        kernel,
        out_shape=(scalar, jax.ShapeDtypeStruct((4 * ROWS, D), F32), jax.ShapeDtypeStruct((ROWS, D), F32), scalar, scalar),
        in_specs=[hbm, hbm, smem, smem],
        out_specs=(smem, vmem, vmem, smem, smem),
        scratch_shapes=[
            V((SIDE, D), BF16), V((SIDE, D), BF16), V((SIDE, SIDE), BF16), V((4 * ROWS, HALF), F32),
            V((SIDE, D), F32), V((SIDE, D), F32), V((SIDE // 2, D), F32),
            V((SIDE, 128), jnp.int32), V((8, SIDE), jnp.int32),
            V((480, 16, 128), BF16), V((540, 16, 128), BF16), V((21, 10, 16, 128), BF16), V((21, 10, 16, 128), BF16),
            V((4, 24, 128), F32), V((4, 24, 128), F32), V((4, 24, 128), F32), V((8, 24, 128), F32),
            V((24, 128), F32), V((24, 128), F32),
            pltpu.SemaphoreType.DMA((sems,)), pltpu.SemaphoreType.DMA((sems,)), pltpu.SemaphoreType.DMA((3,)),
        ],
        compiler_params=pltpu.CompilerParams(collective_id=0, has_side_effects=True, vmem_limit_bytes=48 << 20),
        name="pairs",
    )(images, texts, log_temp, bias)


def solution(mesh):
    return jax.shard_map(
        local,
        mesh=mesh,
        in_specs=(P("grp", None), P(("blk", "grp"), None), P(), P()),
        out_specs=(P(), P("grp", None), P(("blk", "grp"), None), P(), P()),
        check_vma=False,
    )
```
